32 devices in a mesh: dp: 4 (over x, core), expert: 8 (over z, y).
Axes of the slice: x: 2, y: 2, z: 4, core: 2. Of those that a mesh axis runs over, the one named last changes fastest.
Arguments:
- tokens: bfloat16 [1024, 3584], P(('dp', 'expert')), may hold values from -6 to 6
- expert_ids: int32 [1024, 2], P(('dp', 'expert')), may hold values from 0 to 7, all different within a row; in each aligned block of 32 rows (0 to 31, 32 to 63, ...) at most 12 rows name the same one
- mix_weights: float32 [1024, 2], P(('dp', 'expert')), may hold values from 0.25 to 1
- w_up: bfloat16 [8, 3584, 3072], P('expert', None, 'dp'), may hold values from -0.09375 to 0.09375
- w_down: bfloat16 [8, 3072, 3584], P('expert', 'dp'), may hold values from -0.109375 to 0.109375
- out_grad: bfloat16 [1024, 3584], P(('dp', 'expert')), may hold values from -3 to 3
Outputs:
- layer_out: bfloat16 [1024, 3584], P(('dp', 'expert'))
- token_grad: bfloat16 [1024, 3584], P(('dp', 'expert'))
- up_grad: bfloat16 [8, 3584, 3072], P('expert', None, 'dp')
- down_grad: bfloat16 [8, 3072, 3584], P('expert', 'dp')
The draws below stay inside these ranges and needn't reach their ends.
Inputs may be any that keep to these rules, and one draw needn't show every extreme that they name: `expert_ids`: the two experts of a token differ. The 32 tokens of one device name one expert at most 12 times, and in every draw some device names some expert exactly 12 times.
All inputs are finite; a program needn't handle non-finite values.
Results may differ from the reference program's by a relative error of at most 0.015.
Values may be sent and summed in bfloat16 or wider, within the bound.
A program may use at most 128 MiB of HBM per device.

```python
import math
import jax
import jax.numpy as jnp
import numpy as np
from jax import lax

D = 3584
FF = 3072
TOK_DEV = 32
EXPERTS = 8
CAP = 12
TOKENS = 1024
N_DP = 4
N_EXPERT = 8


def block_scale(own_key, extent, shards, smallest, largest):
    loudness, own = 1.0, jax.random.fold_in(own_key, 6)
    for dim, parts in shards:
        heights = jnp.exp(jax.random.uniform(jax.random.fold_in(own, dim), (parts,), jnp.float32, smallest / len(shards), largest / len(shards)))
        loudness = loudness * jnp.repeat(heights, extent[dim] // parts).reshape([-1 if axis == dim else 1 for axis in range(len(extent))])
    return loudness


def deal_out(rng, own, number, rows, count, top, bound, skew):
    sequence = jax.random.permutation(rng, count)
    packed, ordinary = load_shares(count, rows * top, bound, skew, True), load_shares(count, rows * top, bound, skew, False)
    places = jnp.arange(count)

    def named(lengths, rotation):
        used = int((lengths > 0).sum())
        fixed = max(1, used // 4)
        shifted = fixed + (places - fixed + rotation * (used - fixed)) % max(1, count - fixed)
        return jnp.zeros((count,), jnp.int32).at[sequence[jnp.where(places < fixed, places, shifted)]].set(jnp.asarray(lengths, jnp.int32))

    lengths = jnp.where(number % 4 == 0, named(packed, number // 4), named(ordinary, number - number // 4 - 1))
    mixed = jax.random.permutation(jax.random.fold_in(own, 3), count)
    donor, taker = mixed[0:count // 2 * 2:2], mixed[1:count // 2 * 2:2]
    margin = jnp.minimum(lengths[donor] - 1, bound - lengths[taker]) // 2
    margin = jnp.where((donor == sequence[0]) | (taker == sequence[0]) | (lengths[taker] == 0), 0, jnp.maximum(margin, 0))
    shifted = jax.random.randint(jax.random.fold_in(own, 4), (count // 2,), 0, 1 << 20) % (margin + 1)
    lengths = lengths.at[donor].add(-shifted).at[taker].add(shifted)
    labels = jnp.searchsorted(jnp.cumsum(lengths), jnp.arange(rows * top), side="right").astype(jnp.int32)
    grid = labels.reshape(top, rows).T
    grid = grid[jax.random.permutation(jax.random.fold_in(own, 1), rows)]
    rotation = jax.random.randint(jax.random.fold_in(own, 2), (rows, 1), 0, top)
    return jnp.take_along_axis(grid, (jnp.arange(top)[None, :] + rotation) % top, axis=1)


def load_shares(number_of, total, most, slope, full):
    portions = [(1 << 20) // math.isqrt(standing ** slope) + 1 for standing in range(1, number_of + 1)]
    largest = most if full else min(most, max(-(-total // number_of), total * portions[0] // sum(portions)))
    least = 1 if total - largest >= number_of - 1 else 0
    given, surplus = [largest] + [least] * (number_of - 1), total - largest - least * (number_of - 1)
    while surplus > 0:
        candidates = [i for i in range(1, number_of) if given[i] < largest] or [i for i in range(1, number_of) if given[i] < most]
        mass, budget = sum([portions[i] for i in candidates]), surplus
        for i in candidates:
            addition = min(most - given[i], max(1, budget * portions[i] // mass), surplus)
            given[i] = given[i] + addition
            surplus = surplus - addition
    return np.array(given)


def gaussian(key, extent, deviation, most, pieces=(), kind=jnp.bfloat16):
    entries = deviation * jax.random.normal(key, extent, jnp.float32)
    if pieces:
        entries = entries * block_scale(key, extent, pieces, -0.22, 0.18)
    return jnp.clip(entries, -most, most).astype(kind)


def setup_inputs(seed: int = 0) -> dict:
    keys = jax.random.split(jax.random.key(seed), 7)
    tokens = gaussian(keys[0], (TOKENS, D), 1.0, 6.0, ((0, 32),))
    expert_ids_keys = jax.random.split(jax.random.fold_in(keys[1], 1), TOKENS // TOK_DEV)
    expert_ids_turns = jax.random.permutation(jax.random.fold_in(keys[1], 3), TOKENS // TOK_DEV)
    expert_ids = jax.vmap(lambda own, number: deal_out(jax.random.fold_in(keys[1], 2), own, number, TOK_DEV, EXPERTS, 2, CAP, 2))(expert_ids_keys, expert_ids_turns).reshape((TOKENS, 2))
    mix_weights = jnp.clip(0.25 + 0.75 * jax.random.uniform(keys[2], (TOKENS, 2), jnp.float32) ** block_scale(keys[2], (TOKENS, 2), ((0, 32),), -0.2, 0.2), 0.25, 1.0)
    w_up = gaussian(keys[3], (EXPERTS, D, FF), D ** -0.5, 0.09375, ((0, 8), (2, 4)))
    w_down = gaussian(keys[4], (EXPERTS, FF, D), FF ** -0.5, 0.109375, ((0, 8), (1, 4)))
    out_grad = gaussian(keys[5], (TOKENS, D), 0.5, 3.0, ((0, 32),))
    return dict(tokens=tokens, expert_ids=expert_ids, mix_weights=mix_weights, w_up=w_up, w_down=w_down, out_grad=out_grad)


def reference(tokens, expert_ids, mix_weights, w_up, w_down, out_grad):
    row_bound = N_DP * N_EXPERT * CAP
    block_width = FF // N_DP
    pair_ids = expert_ids.reshape(-1)
    pair_weights = mix_weights.reshape(-1).astype(jnp.float32)

    def per_expert(carry, expert):
        out_total, grad_total = carry
        hits = pair_ids == expert
        chosen = jnp.nonzero(hits, size=row_bound, fill_value=0)[0].astype(jnp.int32)
        live = jnp.arange(row_bound, dtype=jnp.int32) < jnp.sum(hits.astype(jnp.int32))
        token_index = (chosen // 2).astype(jnp.int32)
        weight = jnp.where(live, pair_weights[chosen], jnp.zeros((), jnp.float32))
        rows = jnp.where(live[:, None], tokens[token_index], jnp.zeros((), tokens.dtype))
        up_matrix = w_up[expert]
        down_matrix = w_down[expert]
        pre_act = jnp.dot(rows, up_matrix, preferred_element_type=jnp.float32)
        squash = jax.nn.sigmoid(pre_act)
        hidden = (pre_act * squash).astype(jnp.bfloat16)
        block_parts = jnp.einsum("rnk,nkd->rnd", hidden.reshape(row_bound, N_DP, block_width).astype(jnp.float32), down_matrix.reshape(N_DP, block_width, D).astype(jnp.float32))
        rounded = lax.optimization_barrier(block_parts.astype(jnp.bfloat16))
        expert_out = jnp.sum(rounded.astype(jnp.float32), axis=1).astype(jnp.bfloat16)
        out_total = out_total.at[token_index].add(weight[:, None] * expert_out.astype(jnp.float32))
        out_scaled = (weight[:, None] * out_grad[token_index].astype(jnp.float32)).astype(jnp.bfloat16)
        hidden_grad = jnp.dot(out_scaled, down_matrix.T, preferred_element_type=jnp.float32)
        down_part = jnp.dot(hidden.T, out_scaled, preferred_element_type=jnp.float32).astype(jnp.bfloat16)
        pre_grad = (hidden_grad * squash * (1.0 + pre_act * (1.0 - squash))).astype(jnp.bfloat16)
        up_part = jnp.dot(rows.T, pre_grad, preferred_element_type=jnp.float32).astype(jnp.bfloat16)
        grad_parts = jnp.einsum("rnk,dnk->rnd", pre_grad.reshape(row_bound, N_DP, block_width).astype(jnp.float32), up_matrix.reshape(D, N_DP, block_width).astype(jnp.float32))
        grad_rounded = lax.optimization_barrier(grad_parts.astype(jnp.bfloat16))
        pair_grad = jnp.sum(grad_rounded.astype(jnp.float32), axis=1).astype(jnp.bfloat16)
        grad_total = grad_total.at[token_index].add(pair_grad.astype(jnp.float32))
        return (out_total, grad_total), (up_part, down_part)

    start_state = (jnp.zeros((TOKENS, D), jnp.float32), jnp.zeros((TOKENS, D), jnp.float32))
    (out_total, grad_total), (up_grad, down_grad) = lax.scan(per_expert, start_state, jnp.arange(EXPERTS, dtype=jnp.int32))
    return (out_total.astype(jnp.bfloat16), grad_total.astype(jnp.bfloat16), up_grad, down_grad)
```

```python
import functools

import jax
import jax.numpy as jnp
import numpy as np
from jax import lax
from jax.experimental import pallas as pl
from jax.experimental.pallas import tpu as pltpu
from jax.sharding import PartitionSpec as P

MESH = pl.DeviceIdType.MESH
F32 = jnp.float32
BF16 = jnp.bfloat16
CHUNKS = 4


def contract(a, b, da, db):
    return lax.dot_general(a, b, (((da,), (db,)), ((), ())), preferred_element_type=F32)


def kernel(
    n_dp, n_ex, cap,
    ids_ref, mix_ref, tok_ref, og_ref, perm_ref, perm_t_ref, up_hbm, down_hbm,
    lay_ref, tg_ref, up_out, down_out,
    place, up_v, down_v, send, gath, part, pre_act, hidden, pre_grad,
    pair_in, cross_in, back_in,
    w_sem, a_snd, a_rcv, x_snd, x_rcv, p_snd, p_rcv,
    c_snd, c_rcv, r_snd, r_rcv, b_snd, b_rcv, out_sem,
):
    toks = tok_ref.shape[0]
    chunk = gath.shape[-1]
    block = CHUNKS * cap
    slots = n_ex * block
    group = n_ex * cap
    n_x = n_dp // 2
    dp = lax.axis_index("dp")
    ex = lax.axis_index("expert")
    x = dp // 2
    core = dp % 2
    mate = 2 * x + (1 - core)

    def xpeer(o):
        return 2 * ((x + o) % n_x) + core

    def xsource(o):
        return (x + n_x - o) % n_x

    barrier = pltpu.get_barrier_semaphore()
    for o in range(1, n_ex):
        pl.semaphore_signal(barrier, inc=1, device_id=(dp, (ex + o) % n_ex), device_id_type=MESH)
    for o in range(1, n_x):
        pl.semaphore_signal(barrier, inc=1, device_id=(xpeer(o), ex), device_id_type=MESH)
    pl.semaphore_signal(barrier, inc=1, device_id=(mate, ex), device_id_type=MESH)

    up_load = pltpu.make_async_copy(up_hbm, up_v, w_sem.at[0])
    down_load = pltpu.make_async_copy(down_hbm, down_v, w_sem.at[1])
    up_load.start()
    down_load.start()

    lower = (
        lax.broadcasted_iota(jnp.int32, (toks, toks), 1)
        < lax.broadcasted_iota(jnp.int32, (toks, toks), 0)
    )
    lower = jnp.where(lower, 1.0, 0.0).astype(BF16)
    lane = lax.broadcasted_iota(jnp.int32, (toks, n_ex), 1)
    id0, id1 = ids_ref[:, 0:1], ids_ref[:, 1:2]
    hit0 = jnp.where(lane == id0, 1.0, 0.0)
    hit1 = jnp.where(lane == id1, 1.0, 0.0)
    before0 = jnp.dot(lower, hit0.astype(BF16), preferred_element_type=F32)
    before1 = jnp.dot(lower, hit1.astype(BF16), preferred_element_type=F32) + jnp.sum(
        hit0, axis=0, keepdims=True
    )
    pos0 = jnp.sum(before0 * hit0, axis=1, keepdims=True).astype(jnp.int32)
    pos1 = jnp.sum(before1 * hit1, axis=1, keepdims=True).astype(jnp.int32)
    slot = lax.broadcasted_iota(jnp.int32, (toks, slots), 1)
    for k, (ids, pos) in enumerate(((id0, pos0), (id1, pos1))):
        for c in range(CHUNKS):
            hit = slot == ids * block + pos + c * cap
            place[k, c * toks:(c + 1) * toks, :] = jnp.where(hit, 1.0, 0.0).astype(BF16)

    def rows_of(e):
        return pl.ds(pl.multiple_of(e * block, 16), block)

    def stacked(value):
        return jnp.concatenate(
            [value[:, c * chunk:(c + 1) * chunk] for c in range(CHUNKS)], axis=0
        )

    def a2a(s, o, to):
        src = (ex + o) % n_ex
        return pltpu.make_async_remote_copy(
            src_ref=send.at[s, rows_of(src)],
            dst_ref=gath.at[s, dp, rows_of(to)],
            send_sem=a_snd.at[s, o], recv_sem=a_rcv.at[s, o],
            device_id=(dp, src), device_id_type=MESH,
        )

    def forward_x(s, ox, o):
        src = (ex + n_ex - o) % n_ex
        return pltpu.make_async_remote_copy(
            src_ref=gath.at[s, dp, rows_of(src)],
            dst_ref=gath.at[s, dp, rows_of(src)],
            send_sem=x_snd.at[s, ox, o], recv_sem=x_rcv.at[s, ox, o],
            device_id=(xpeer(ox), ex), device_id_type=MESH,
        )

    def arrived_x(s, ox, o):
        src = (ex + n_ex - o) % n_ex
        owner = 2 * xsource(ox) + core
        return pltpu.make_async_remote_copy(
            src_ref=gath.at[s, owner, rows_of(src)],
            dst_ref=gath.at[s, owner, rows_of(src)],
            send_sem=x_snd.at[s, ox, o], recv_sem=x_rcv.at[s, ox, o],
            device_id=(xpeer(ox), ex), device_id_type=MESH,
        )

    def mate_copy(s, ox, o, half):
        src = (ex + n_ex - o) % n_ex
        owner = 2 * xsource(ox) + half
        return pltpu.make_async_remote_copy(
            src_ref=gath.at[s, owner, rows_of(src)],
            dst_ref=gath.at[s, owner, rows_of(src)],
            send_sem=p_snd.at[s, ox, o], recv_sem=p_rcv.at[s, ox, o],
            device_id=(mate, ex), device_id_type=MESH,
        )

    def launch(s):
        gath[s, dp, rows_of(ex), :] = send[s, rows_of(ex), :]

        @pl.loop(1, n_ex)
        def _(o):
            a2a(s, o, ex).start()

    def spread_own(s, o):
        for ox in range(1, n_x):
            forward_x(s, ox, o).start()
        mate_copy(s, 0, o, core).start()

    def spread_cross(s, o):
        for ox in range(1, n_x):
            arrived_x(s, ox, o).wait_recv()
            mate_copy(s, ox, o, core).start()

    def own_arrival(s, o):
        a2a(s, o, (ex + n_ex - o) % n_ex).wait_recv()
        spread_own(s, o)

    def gathered(s):
        @pl.loop(0, n_ex)
        def _(o):
            for ox in range(n_x):
                mate_copy(s, ox, o, 1 - core).wait_recv()
                mate_copy(s, ox, o, core).wait_send()
            for ox in range(1, n_x):
                forward_x(s, ox, o).wait_send()

        @pl.loop(0, n_dp)
        def _(d):
            moved = jnp.dot(perm_ref[...], gath[s, d], preferred_element_type=F32)
            gath[s, d] = moved.astype(BF16)

    def piece(s, c):
        rows = pl.ds(pl.multiple_of(c * group, 16), group)
        return jnp.concatenate([gath[s, d, rows, :] for d in range(n_dp)], axis=0)

    def put_part(s, c, value):
        rows = pl.ds(pl.multiple_of(c * group, 16), group)
        for d in range(n_dp):
            part[s, d, rows, :] = value[d * group:(d + 1) * group]

    def cols(c):
        return pl.ds(pl.multiple_of(c * chunk, 128), chunk)

    def pair_copy(s, xi):
        return pltpu.make_async_remote_copy(
            src_ref=part.at[s, 2 * xi + (1 - core)], dst_ref=pair_in.at[s, xi],
            send_sem=c_snd.at[s, xi], recv_sem=c_rcv.at[s, xi],
            device_id=(mate, ex), device_id_type=MESH,
        )

    def cross_copy(s, ox):
        return pltpu.make_async_remote_copy(
            src_ref=part.at[s, xpeer(ox)], dst_ref=cross_in.at[s, ox - 1],
            send_sem=r_snd.at[s, ox], recv_sem=r_rcv.at[s, ox],
            device_id=(xpeer(ox), ex), device_id_type=MESH,
        )

    def pair_sum(s):
        for ox in [*range(1, n_x), 0]:
            xi = (x + ox) % n_x
            pair_copy(s, xi).wait_recv()
            mine = 2 * xi + core
            total = part[s, mine].astype(F32) + pair_in[s, xi].astype(F32)
            part[s, mine] = total.astype(BF16)
            if ox:
                cross_copy(s, ox).start()

    def back_copy(s, o, to):
        dest = (ex + o) % n_ex
        return pltpu.make_async_remote_copy(
            src_ref=send.at[s, rows_of(dest)], dst_ref=back_in.at[s, rows_of(to)],
            send_sem=b_snd.at[s, o], recv_sem=b_rcv.at[s, o],
            device_id=(dp, dest), device_id_type=MESH,
        )

    def send_back(s):
        total = part[s, dp].astype(F32)
        for ox in range(1, n_x):
            cross_copy(s, ox).wait_recv()
            total = total + cross_in[s, ox - 1].astype(F32)

        @pl.loop(1, n_ex)
        def _(o):
            a2a(s, o, ex).wait_send()

        moved = jnp.dot(perm_t_ref[...], total.astype(BF16), preferred_element_type=F32)
        send[s] = moved.astype(BF16)
        back_in[s, rows_of(ex), :] = send[s, rows_of(ex), :]

        @pl.loop(1, n_ex)
        def _(o):
            back_copy(s, o, ex).start()

    def returned(s):
        @pl.loop(1, n_ex)
        def _(o):
            back_copy(s, o, (ex + n_ex - o) % n_ex).wait_recv()

    both = place[0] + place[1]
    send[0] = contract(both, stacked(tok_ref[...]), 0, 0).astype(BF16)
    pl.semaphore_wait(barrier, n_ex - 1 + n_x)
    launch(0)
    og = og_ref[...].astype(F32)
    scaled0 = stacked((og * mix_ref[:, 0:1]).astype(BF16))
    scaled1 = stacked((og * mix_ref[:, 1:2]).astype(BF16))
    send[1] = (contract(place[0], scaled0, 0, 0) + contract(place[1], scaled1, 0, 0)).astype(BF16)
    launch(1)

    spread_own(0, 0)

    @pl.loop(1, n_ex)
    def _(o):
        own_arrival(0, o)

    spread_own(1, 0)
    spread_cross(0, 0)

    @pl.loop(1, n_ex)
    def _(o):
        own_arrival(1, o)
        spread_cross(0, o)

    gathered(0)
    up_load.wait()
    pre_act[...] = jnp.zeros_like(pre_act)

    @pl.loop(0, CHUNKS)
    def _(c):
        pre_act[...] += jnp.dot(piece(0, c), up_v[cols(c), :], preferred_element_type=F32)

    act = pre_act[...]
    hidden[...] = (act * jax.nn.sigmoid(act)).astype(BF16)
    down_load.wait()

    @pl.loop(0, CHUNKS)
    def _(c):
        put_part(0, c, jnp.dot(hidden[...], down_v[:, cols(c)], preferred_element_type=F32).astype(BF16))

    for xi in range(n_x):
        pair_copy(0, xi).start()

    @pl.loop(0, n_ex)
    def _(o):
        spread_cross(1, o)

    pair_sum(0)
    gathered(1)

    act = pre_act[...]
    squash = jax.nn.sigmoid(act)
    pre_act[...] = jnp.zeros_like(pre_act)

    @pl.loop(0, CHUNKS)
    def _(c):
        pre_act[...] += contract(piece(1, c), down_v[:, cols(c)], 1, 1)

    pre_grad[...] = (pre_act[...] * (squash * (1.0 + act * (1.0 - squash)))).astype(BF16)

    @pl.loop(0, CHUNKS)
    def _(c):
        put_part(1, c, contract(pre_grad[...], up_v[cols(c), :], 1, 1).astype(BF16))

    for xi in range(n_x):
        pair_copy(1, xi).start()
    send_back(0)
    pair_sum(1)

    def up_store(c):
        return pltpu.make_async_copy(up_v.at[cols(c), :], up_out.at[cols(c), :], out_sem.at[0, c])

    def down_store(c):
        return pltpu.make_async_copy(down_v.at[:, cols(c)], down_out.at[:, cols(c)], out_sem.at[1, c])

    @pl.loop(0, CHUNKS)
    def _(c):
        up_v[cols(c), :] = contract(piece(0, c), pre_grad[...], 0, 0).astype(BF16)
        up_store(c).start()

    send_back(1)

    @pl.loop(0, CHUNKS)
    def _(c):
        down_v[:, cols(c)] = contract(hidden[...], piece(1, c), 0, 0).astype(BF16)
        down_store(c).start()

    returned(0)
    weight = (
        place[0].astype(F32) * jnp.concatenate([mix_ref[:, 0:1]] * CHUNKS, axis=0)
        + place[1].astype(F32) * jnp.concatenate([mix_ref[:, 1:2]] * CHUNKS, axis=0)
    )
    high = weight.astype(BF16)
    low = (weight - high.astype(F32)).astype(BF16)
    value = back_in[0]
    out = jnp.dot(high, value, preferred_element_type=F32) + jnp.dot(
        low, value, preferred_element_type=F32
    )
    for c in range(CHUNKS):
        lay_ref[:, c * chunk:(c + 1) * chunk] = out[c * toks:(c + 1) * toks].astype(BF16)
    returned(1)
    out = jnp.dot(place[0] + place[1], back_in[1], preferred_element_type=F32)
    for c in range(CHUNKS):
        tg_ref[:, c * chunk:(c + 1) * chunk] = out[c * toks:(c + 1) * toks].astype(BF16)

    for s in range(2):
        @pl.loop(1, n_ex)
        def _(o):
            back_copy(s, o, ex).wait_send()

        for xi in range(n_x):
            pair_copy(s, xi).wait_send()
        for ox in range(1, n_x):
            cross_copy(s, ox).wait_send()

    @pl.loop(0, CHUNKS)
    def _(c):
        up_store(c).wait()
        down_store(c).wait()


def per_device(tokens, expert_ids, mix_weights, w_up, w_down, out_grad):
    toks, width = tokens.shape
    n_dp, n_ex = lax.axis_size("dp"), lax.axis_size("expert")
    hid = w_up.shape[2]
    limit = max(2, 3 * toks // n_ex)
    cap = -(-limit // 4) * 4
    chunk = width // CHUNKS
    block = CHUNKS * cap
    slots, group = n_ex * block, n_ex * cap
    rows = n_dp * group
    n_x = n_dp // 2
    perm = np.zeros((slots, slots), np.float32)
    for c in range(CHUNKS):
        for e in range(n_ex):
            for s in range(cap):
                perm[c * group + e * cap + s, e * block + c * cap + s] = 1
    vmem = pl.BlockSpec(memory_space=pltpu.VMEM)
    hbm = pl.BlockSpec(memory_space=pl.ANY)
    dma = pltpu.SemaphoreType.DMA
    cross = max(1, n_x - 1)
    layer_out, token_grad, up_grad, down_grad = pl.pallas_call(
        functools.partial(kernel, n_dp, n_ex, cap),
        out_shape=(
            jax.ShapeDtypeStruct((toks, width), BF16),
            jax.ShapeDtypeStruct((toks, width), BF16),
            jax.ShapeDtypeStruct((width, hid), BF16),
            jax.ShapeDtypeStruct((hid, width), BF16),
        ),
        in_specs=[vmem] * 6 + [hbm] * 2,
        out_specs=(vmem, vmem, hbm, hbm),
        scratch_shapes=[
            pltpu.VMEM((2, CHUNKS * toks, slots), BF16),
            pltpu.VMEM((width, hid), BF16),
            pltpu.VMEM((hid, width), BF16),
            pltpu.VMEM((2, slots, chunk), BF16),
            pltpu.VMEM((2, n_dp, slots, chunk), BF16),
            pltpu.VMEM((2, n_dp, slots, chunk), BF16),
            pltpu.VMEM((rows, hid), F32),
            pltpu.VMEM((rows, hid), BF16),
            pltpu.VMEM((rows, hid), BF16),
            pltpu.VMEM((2, n_x, slots, chunk), BF16),
            pltpu.VMEM((2, cross, slots, chunk), BF16),
            pltpu.VMEM((2, slots, chunk), BF16),
            dma((2,)),
            dma((2, n_ex)), dma((2, n_ex)),
            dma((2, n_x, n_ex)), dma((2, n_x, n_ex)),
            dma((2, n_x, n_ex)), dma((2, n_x, n_ex)),
            dma((2, n_x)), dma((2, n_x)),
            dma((2, n_x)), dma((2, n_x)),
            dma((2, n_ex)), dma((2, n_ex)),
            dma((2, CHUNKS)),
        ],
        compiler_params=pltpu.CompilerParams(
            collective_id=0, has_side_effects=True, vmem_limit_bytes=62 * 1024 * 1024
        ),
        cost_estimate=pl.CostEstimate(
            flops=12 * rows * width * hid,
            bytes_accessed=8 * width * hid,
            transcendentals=2 * rows * hid,
        ),
    )(
        expert_ids, mix_weights, tokens, out_grad,
        jnp.asarray(perm, BF16), jnp.asarray(perm.T, BF16), w_up[0], w_down[0],
    )
    return layer_out, token_grad, up_grad[None], down_grad[None]


def solution(mesh):
    in_specs = (
        P(("dp", "expert"), None),
        P(("dp", "expert"), None),
        P(("dp", "expert"), None),
        P("expert", None, "dp"),
        P("expert", "dp", None),
        P(("dp", "expert"), None),
    )
    out_specs = (
        P(("dp", "expert"), None),
        P(("dp", "expert"), None),
        P("expert", None, "dp"),
        P("expert", "dp", None),
    )
    return jax.shard_map(
        per_device, mesh=mesh, in_specs=in_specs, out_specs=out_specs, check_vma=False
    )
```

```python
import functools

import jax
import jax.numpy as jnp
import numpy as np
from jax import lax
from jax.experimental import pallas as pl
from jax.experimental.pallas import tpu as pltpu
from jax.sharding import PartitionSpec as P

MESH = pl.DeviceIdType.MESH
F32 = jnp.float32
BF16 = jnp.bfloat16
CHUNKS = 4


def contract(a, b, da, db):
    return lax.dot_general(a, b, (((da,), (db,)), ((), ())), preferred_element_type=F32)


def kernel(
    n_dp, n_ex, cap,
    ids_ref, mix_ref, tok_ref, og_ref, perm_ref, perm_t_ref, up_hbm, down_hbm,
    lay_ref, tg_ref, up_out, down_out,
    place, up_v, down_v, send, gath, part, pre_act, hidden, pre_grad,
    pair_in, cross_in, back_in,
    w_sem, a_snd, a_rcv, x_snd, x_rcv, p_snd, p_rcv,
    c_snd, c_rcv, r_snd, r_rcv, b_snd, b_rcv, out_sem,
):
    toks = tok_ref.shape[0]
    chunk = gath.shape[-1]
    block = CHUNKS * cap
    slots = n_ex * block
    group = n_ex * cap
    n_x = n_dp // 2
    dp = lax.axis_index("dp")
    ex = lax.axis_index("expert")
    x = dp // 2
    core = dp % 2
    mate = 2 * x + (1 - core)

    bits = [1 << i for i in range(n_ex.bit_length() - 1)]

    def xpeer(o):
        return 2 * ((x + o) % n_x) + core

    def xsource(o):
        return (x + n_x - o) % n_x

    barrier = pltpu.get_barrier_semaphore()
    for o in range(1, n_ex):
        pl.semaphore_signal(barrier, inc=1, device_id=(dp, (ex + o) % n_ex), device_id_type=MESH)
    for o in range(1, n_x):
        pl.semaphore_signal(barrier, inc=1, device_id=(xpeer(o), ex), device_id_type=MESH)
    pl.semaphore_signal(barrier, inc=1, device_id=(mate, ex), device_id_type=MESH)

    up_load = pltpu.make_async_copy(up_hbm, up_v, w_sem.at[0])
    down_load = pltpu.make_async_copy(down_hbm, down_v, w_sem.at[1])
    up_load.start()
    down_load.start()

    wide = CHUNKS * toks

    def iota(shape, dim):
        return lax.broadcasted_iota(jnp.int32, shape, dim)

    def ones(where):
        return jnp.where(where, 1.0, 0.0)

    earlier = ones(iota((toks, toks), 0) < iota((toks, toks), 1)).astype(BF16)
    tile = sum(
        ones(iota((toks, wide), 1) == iota((toks, wide), 0) + c * toks) for c in range(CHUNKS)
    ).astype(BF16)

    def tiled(row):
        full = jnp.broadcast_to(row, (8, toks)).astype(BF16)
        return jnp.dot(full, tile, preferred_element_type=F32)[0:1]

    hits = [ones(iota((n_ex, toks), 0) == ids_ref[k:k + 1, :]) for k in range(2)]
    before = [jnp.dot(hit.astype(BF16), earlier, preferred_element_type=F32) for hit in hits]
    before[1] = before[1] + jnp.sum(hits[0], axis=1, keepdims=True)
    ids = ids_ref[...]
    rank_ids = ((ids >> 1) & 1) * (n_ex // 2) + (ids >> 2) * 2 + (ids & 1)
    lane_chunk = sum(jnp.where(iota((1, wide), 1) >= c * toks, 1, 0) for c in range(1, CHUNKS))
    for k in range(2):
        pos = jnp.sum(before[k] * hits[k], axis=0, keepdims=True)
        target = tiled(rank_ids[k:k + 1, :].astype(F32)) * block + tiled(pos)
        target = target.astype(jnp.int32) + lane_chunk * cap
        place[k] = ones(iota((slots, wide), 0) == target).astype(BF16)

    def rank(e):
        return (e // 2) % 2 * (n_ex // 2) + e // 4 * 2 + e % 2

    def rows_of(e):
        return pl.ds(pl.multiple_of(rank(e) * block, 16), block)

    def half_rows(h):
        return pl.ds(h * (slots // 2), slots // 2)

    def swap(o):
        return sum((ex // bit + o // bit) % 2 * bit for bit in bits)

    def stacked(value):
        return jnp.concatenate(
            [value[:, c * chunk:(c + 1) * chunk] for c in range(CHUNKS)], axis=0
        )

    def a2a(s, o, to):
        src = swap(o)
        return pltpu.make_async_remote_copy(
            src_ref=send.at[s, rows_of(src)],
            dst_ref=gath.at[s, dp, rows_of(to)],
            send_sem=a_snd.at[s, o], recv_sem=a_rcv.at[s, o],
            device_id=(dp, src), device_id_type=MESH,
        )

    def forward_x(s, ox, o):
        src = swap(o)
        return pltpu.make_async_remote_copy(
            src_ref=gath.at[s, dp, rows_of(src)],
            dst_ref=gath.at[s, dp, rows_of(src)],
            send_sem=x_snd.at[s, ox, o], recv_sem=x_rcv.at[s, ox, o],
            device_id=(xpeer(ox), ex), device_id_type=MESH,
        )

    def arrived_x(s, ox, o):
        src = swap(o)
        owner = 2 * xsource(ox) + core
        return pltpu.make_async_remote_copy(
            src_ref=gath.at[s, owner, rows_of(src)],
            dst_ref=gath.at[s, owner, rows_of(src)],
            send_sem=x_snd.at[s, ox, o], recv_sem=x_rcv.at[s, ox, o],
            device_id=(xpeer(ox), ex), device_id_type=MESH,
        )

    def mate_copy(s, ox, o, half):
        src = swap(o)
        owner = 2 * xsource(ox) + half
        return pltpu.make_async_remote_copy(
            src_ref=gath.at[s, owner, rows_of(src)],
            dst_ref=gath.at[s, owner, rows_of(src)],
            send_sem=p_snd.at[s, ox, o], recv_sem=p_rcv.at[s, ox, o],
            device_id=(mate, ex), device_id_type=MESH,
        )

    def keep_own(s):
        gath[s, dp, rows_of(ex), :] = send[s, rows_of(ex), :]

    def spread_own(s, o):
        for ox in range(1, n_x):
            forward_x(s, ox, o).start()
        mate_copy(s, 0, o, core).start()

    def spread_cross(s, o):
        for ox in range(1, n_x):
            arrived_x(s, ox, o).wait_recv()
            mate_copy(s, ox, o, core).start()

    def own_arrival(s, o):
        a2a(s, o, swap(o)).wait_recv()
        spread_own(s, o)

    def gathered(s):
        @pl.loop(0, n_ex)
        def _(o):
            for ox in range(n_x):
                mate_copy(s, ox, o, 1 - core).wait_recv()
                mate_copy(s, ox, o, core).wait_send()
            for ox in range(1, n_x):
                forward_x(s, ox, o).wait_send()

        @pl.loop(0, n_dp)
        def _(d):
            for h in range(2):
                moved = jnp.dot(perm_ref[...], gath[s, d, half_rows(h), :], preferred_element_type=F32)
                gath[s, d, half_rows(h), :] = moved.astype(BF16)

    def strips(c):
        return [
            pl.ds(pl.multiple_of(h * (slots // 2) + c * (group // 2), 16), group // 2)
            for h in range(2)
        ]

    def piece(s, c):
        return jnp.concatenate(
            [gath[s, d, rows, :] for d in range(n_dp) for rows in strips(c)], axis=0
        )

    def put_part(s, c, value):
        size = group // 2
        for d in range(n_dp):
            for h, rows in enumerate(strips(c)):
                at = (2 * d + h) * size
                part[s, d, rows, :] = value[at:at + size]

    def cols(c):
        return pl.ds(pl.multiple_of(c * chunk, 128), chunk)

    def pair_copy(s, xi):
        return pltpu.make_async_remote_copy(
            src_ref=part.at[s, 2 * xi + (1 - core)], dst_ref=pair_in.at[s, xi],
            send_sem=c_snd.at[s, xi], recv_sem=c_rcv.at[s, xi],
            device_id=(mate, ex), device_id_type=MESH,
        )

    def cross_copy(s, ox, h):
        return pltpu.make_async_remote_copy(
            src_ref=part.at[s, xpeer(ox), half_rows(h)],
            dst_ref=cross_in.at[s, ox - 1, half_rows(h)],
            send_sem=r_snd.at[s, ox, h], recv_sem=r_rcv.at[s, ox, h],
            device_id=(xpeer(ox), ex), device_id_type=MESH,
        )

    def pair_sum(s):
        for ox in [*range(1, n_x), 0]:
            xi = (x + ox) % n_x
            pair_copy(s, xi).wait_recv()
            mine = 2 * xi + core
            for h in range(2):
                rows = half_rows(h)
                total = part[s, mine, rows, :].astype(F32) + pair_in[s, xi, rows, :].astype(F32)
                part[s, mine, rows, :] = total.astype(BF16)
                if ox:
                    cross_copy(s, ox, h).start()

    def back_copy(s, source, dest):
        return pltpu.make_async_remote_copy(
            src_ref=send.at[s, rows_of(dest)], dst_ref=back_in.at[s, rows_of(source)],
            send_sem=b_snd.at[s, dest], recv_sem=b_rcv.at[s, source],
            device_id=(dp, dest), device_id_type=MESH,
        )

    def sent(s):
        @pl.loop(1, n_ex)
        def _(o):
            a2a(s, o, ex).wait_send()

    def send_back(s, h):
        rows = half_rows(h)
        total = part[s, dp, rows, :].astype(F32)
        for ox in range(1, n_x):
            cross_copy(s, ox, h).wait_recv()
            total = total + cross_in[s, ox - 1, rows, :].astype(F32)
        moved = jnp.dot(perm_t_ref[...], total.astype(BF16), preferred_element_type=F32)
        send[s, rows, :] = moved.astype(BF16)

        @pl.loop(0, n_ex)
        def _(o):
            dest = swap(o)

            @pl.when(dest // 2 % 2 == h)
            def _():
                @pl.when(o > 0)
                def _():
                    back_copy(s, ex, dest).start()

                @pl.when(o == 0)
                def _():
                    back_in[s, rows_of(ex), :] = send[s, rows_of(ex), :]

    def returned(s):
        @pl.loop(1, n_ex)
        def _(o):
            back_copy(s, swap(o), swap(o)).wait_recv()

    both = place[0] + place[1]
    send[0] = jnp.dot(both, stacked(tok_ref[...]), preferred_element_type=F32).astype(BF16)
    pl.semaphore_wait(barrier, n_ex - 1 + n_x)
    keep_own(0)

    @pl.loop(1, n_ex)
    def _(o):
        a2a(0, o, ex).start()

    spread_own(0, 0)
    og = og_ref[...].astype(F32)
    eye = iota((toks, toks), 0) == iota((toks, toks), 1)
    mixed = []
    for k in range(2):
        column = jnp.sum(jnp.where(eye, mix_ref[k:k + 1, :], 0.0), axis=1, keepdims=True)
        scaled = stacked((og * column).astype(BF16))
        mixed.append(jnp.dot(place[k], scaled, preferred_element_type=F32))
    send[1] = (mixed[0] + mixed[1]).astype(BF16)
    keep_own(1)

    @pl.loop(1, n_ex)
    def _(o):
        own_arrival(0, o)
        a2a(1, o, ex).start()

    spread_own(1, 0)
    spread_cross(0, 0)

    @pl.loop(1, n_ex)
    def _(o):
        own_arrival(1, o)
        spread_cross(0, o)

    gathered(0)
    up_load.wait()
    pre_act[...] = jnp.zeros_like(pre_act)

    @pl.loop(0, CHUNKS)
    def _(c):
        pre_act[...] += jnp.dot(piece(0, c), up_v[cols(c), :], preferred_element_type=F32)

    act = pre_act[...]
    hidden[...] = (act * jax.nn.sigmoid(act)).astype(BF16)
    down_load.wait()

    @pl.loop(0, CHUNKS)
    def _(c):
        put_part(0, c, jnp.dot(hidden[...], down_v[:, cols(c)], preferred_element_type=F32).astype(BF16))

    for xi in range(n_x):
        pair_copy(0, xi).start()

    @pl.loop(0, n_ex)
    def _(o):
        spread_cross(1, o)

    pair_sum(0)
    gathered(1)

    act = pre_act[...]
    squash = jax.nn.sigmoid(act)
    pre_act[...] = jnp.zeros_like(pre_act)

    @pl.loop(0, CHUNKS)
    def _(c):
        pre_act[...] += contract(piece(1, c), down_v[:, cols(c)], 1, 1)

    pre_grad[...] = (pre_act[...] * (squash * (1.0 + act * (1.0 - squash)))).astype(BF16)

    @pl.loop(0, CHUNKS)
    def _(c):
        put_part(1, c, contract(pre_grad[...], up_v[cols(c), :], 1, 1).astype(BF16))

    for xi in range(n_x):
        pair_copy(1, xi).start()
    sent(0)
    send_back(0, 0)
    send_back(0, 1)
    pair_sum(1)

    def up_store(c):
        return pltpu.make_async_copy(up_v.at[cols(c), :], up_out.at[cols(c), :], out_sem.at[0, c])

    def down_store(c):
        return pltpu.make_async_copy(down_v.at[:, cols(c)], down_out.at[:, cols(c)], out_sem.at[1, c])

    @pl.loop(0, CHUNKS)
    def _(c):
        up_v[cols(c), :] = contract(piece(0, c), pre_grad[...], 0, 0).astype(BF16)
        up_store(c).start()

    sent(1)
    send_back(1, 0)

    @pl.loop(0, CHUNKS)
    def _(c):
        down_v[:, cols(c)] = contract(hidden[...], piece(1, c), 0, 0).astype(BF16)
        down_store(c).start()

    send_back(1, 1)
    returned(0)
    high = low = 0.0
    for k in range(2):
        row = mix_ref[k:k + 1, :]
        upper = row.astype(BF16).astype(F32)
        high = high + place[k].astype(F32) * tiled(upper)
        low = low + place[k].astype(F32) * tiled(row - upper)
    value = back_in[0]
    out = contract(high.astype(BF16), value, 0, 0) + contract(low.astype(BF16), value, 0, 0)
    for c in range(CHUNKS):
        lay_ref[:, c * chunk:(c + 1) * chunk] = out[c * toks:(c + 1) * toks].astype(BF16)
    returned(1)
    out = contract(place[0] + place[1], back_in[1], 0, 0)
    for c in range(CHUNKS):
        tg_ref[:, c * chunk:(c + 1) * chunk] = out[c * toks:(c + 1) * toks].astype(BF16)

    for s in range(2):
        @pl.loop(1, n_ex)
        def _(o):
            back_copy(s, ex, swap(o)).wait_send()

        for xi in range(n_x):
            pair_copy(s, xi).wait_send()
        for ox in range(1, n_x):
            for h in range(2):
                cross_copy(s, ox, h).wait_send()

    @pl.loop(0, CHUNKS)
    def _(c):
        up_store(c).wait()
        down_store(c).wait()


def per_device(tokens, expert_ids, mix_weights, w_up, w_down, out_grad):
    toks, width = tokens.shape
    n_dp, n_ex = lax.axis_size("dp"), lax.axis_size("expert")
    hid = w_up.shape[2]
    limit = max(2, 3 * toks // n_ex)
    cap = -(-limit // 4) * 4
    chunk = width // CHUNKS
    block = CHUNKS * cap
    slots, group = n_ex * block, n_ex * cap
    rows = n_dp * group
    n_x = n_dp // 2
    part = n_ex // 2
    perm = np.zeros((slots // 2, slots // 2), np.float32)
    for c in range(CHUNKS):
        for e in range(part):
            for s in range(cap):
                perm[c * part * cap + e * cap + s, e * block + c * cap + s] = 1
    vmem = pl.BlockSpec(memory_space=pltpu.VMEM)
    hbm = pl.BlockSpec(memory_space=pl.ANY)
    dma = pltpu.SemaphoreType.DMA
    cross = max(1, n_x - 1)
    layer_out, token_grad, up_grad, down_grad = pl.pallas_call(
        functools.partial(kernel, n_dp, n_ex, cap),
        out_shape=(
            jax.ShapeDtypeStruct((toks, width), BF16),
            jax.ShapeDtypeStruct((toks, width), BF16),
            jax.ShapeDtypeStruct((width, hid), BF16),
            jax.ShapeDtypeStruct((hid, width), BF16),
        ),
        in_specs=[vmem] * 6 + [hbm] * 2,
        out_specs=(vmem, vmem, hbm, hbm),
        scratch_shapes=[
            pltpu.VMEM((2, slots, CHUNKS * toks), BF16),
            pltpu.VMEM((width, hid), BF16),
            pltpu.VMEM((hid, width), BF16),
            pltpu.VMEM((2, slots, chunk), BF16),
            pltpu.VMEM((2, n_dp, slots, chunk), BF16),
            pltpu.VMEM((2, n_dp, slots, chunk), BF16),
            pltpu.VMEM((rows, hid), F32),
            pltpu.VMEM((rows, hid), BF16),
            pltpu.VMEM((rows, hid), BF16),
            pltpu.VMEM((2, n_x, slots, chunk), BF16),
            pltpu.VMEM((2, cross, slots, chunk), BF16),
            pltpu.VMEM((2, slots, chunk), BF16),
            dma((2,)),
            dma((2, n_ex)), dma((2, n_ex)),
            dma((2, n_x, n_ex)), dma((2, n_x, n_ex)),
            dma((2, n_x, n_ex)), dma((2, n_x, n_ex)),
            dma((2, n_x)), dma((2, n_x)),
            dma((2, n_x, 2)), dma((2, n_x, 2)),
            dma((2, n_ex)), dma((2, n_ex)),
            dma((2, CHUNKS)),
        ],
        compiler_params=pltpu.CompilerParams(
            collective_id=0, has_side_effects=True, vmem_limit_bytes=62 * 1024 * 1024
        ),
        cost_estimate=pl.CostEstimate(
            flops=12 * rows * width * hid,
            bytes_accessed=8 * width * hid,
            transcendentals=2 * rows * hid,
        ),
    )(
        expert_ids.T, mix_weights.T, tokens, out_grad,
        jnp.asarray(perm, BF16), jnp.asarray(perm.T, BF16), w_up[0], w_down[0],
    )
    return layer_out, token_grad, up_grad[None], down_grad[None]


def solution(mesh):
    in_specs = (
        P(("dp", "expert"), None),
        P(("dp", "expert"), None),
        P(("dp", "expert"), None),
        P("expert", None, "dp"),
        P("expert", "dp", None),
        P(("dp", "expert"), None),
    )
    out_specs = (
        P(("dp", "expert"), None),
        P(("dp", "expert"), None),
        P("expert", None, "dp"),
        P("expert", "dp", None),
    )
    return jax.shard_map(
        per_device, mesh=mesh, in_specs=in_specs, out_specs=out_specs, check_vma=False
    )
```
